128 devices in a mesh: fsdp: 2 (over z_hi), ctx: 64 (over z_lo, x, y, core).
Axes of the slice: x: 4, y: 4, z: 4 (z_hi: 2, z_lo: 2; z = z_hi * 2 + z_lo), core: 2. Of those that a mesh axis runs over, the one named last changes fastest.
Arguments:
- tokens: bfloat16 [2, 8192, 768], P('fsdp', 'ctx'), may hold values from -6 to 6
- attn_gain: bfloat16 [768], P('fsdp'), may hold values from 0.099609375 to 1.8984375
- attn_shift: bfloat16 [768], P('fsdp'), may hold values from -1.75 to 1.75
- input_weight: bfloat16 [768, 2304], P('fsdp'), may hold values from -0.21875 to 0.21875
- query_bias: bfloat16 [768], P('fsdp'), may hold values from -3 to 3
- value_bias: bfloat16 [768], P('fsdp'), may hold values from -3 to 3
- output_weight: bfloat16 [768, 768], P('fsdp'), may hold values from -6 to 6
- output_bias: bfloat16 [768], P('fsdp'), may hold values from -1.75 to 1.75
- mlp_gain: bfloat16 [768], P('fsdp'), may hold values from 0.099609375 to 1.8984375
- mlp_shift: bfloat16 [768], P('fsdp'), may hold values from -1.75 to 1.75
- hidden_weight: bfloat16 [768, 3072], P('fsdp'), may hold values from -0.21875 to 0.21875
- hidden_bias: bfloat16 [3072], P('fsdp'), may hold values from -3 to 3
- return_weight: bfloat16 [3072, 768], P('fsdp'), may hold values from -0.109375 to 0.109375
- return_bias: bfloat16 [768], P('fsdp'), may hold values from -1.75 to 1.75
- block_order: int32 [128], replicated, may hold values from 0 to 127, as said below
- cotangent: bfloat16 [2, 8192, 768], P('fsdp', 'ctx'), may hold values from -6 to 6
Outputs:
- layer_out: bfloat16 [2, 8192, 768], P('fsdp', 'ctx')
- tokens_grad: bfloat16 [2, 8192, 768], P('fsdp', 'ctx')
- grad_attn_gain: float32 [768], P('fsdp')
- grad_attn_shift: float32 [768], P('fsdp')
- grad_input_weight: float32 [768, 2304], P('fsdp')
- grad_query_bias: float32 [768], P('fsdp')
- grad_value_bias: float32 [768], P('fsdp')
- grad_output_weight: float32 [768, 768], P('fsdp')
- grad_output_bias: float32 [768], P('fsdp')
- grad_mlp_gain: float32 [768], P('fsdp')
- grad_mlp_shift: float32 [768], P('fsdp')
- grad_hidden_weight: float32 [768, 3072], P('fsdp')
- grad_hidden_bias: float32 [3072], P('fsdp')
- grad_return_weight: float32 [3072, 768], P('fsdp')
- grad_return_bias: float32 [768], P('fsdp')
The draws below stay inside these ranges and needn't reach their ends.
Inputs may be any that keep to these rules, and one draw needn't show every extreme that they name: `block_order`: entries 2 c and 2 c + 1 are the causal blocks held by index c of ctx; the entries are a permutation of the 128 blocks and entries 2 c and 2 c + 1 add up to 127.
All inputs are finite; a program needn't handle non-finite values.
Results may differ from the reference program's by a relative error of at most 0.014.
Values may be sent and summed in bfloat16 or wider, within the bound.
No kernel may reach another device: no remote copies, remote signals or barrier semaphores. Data moves between devices by JAX's collectives and lax.ppermute only.
A program may use at most 256 MiB of HBM per device.

```python
import jax
import jax.numpy as jnp
from jax import lax

D = 768
H = 12
HEAD_DIM = 64
FF = 3072
BLK = 64
SEQ_LEN = 8192
SEQS_ALL = 2
BLOCKS = 128


def draw_block_order(key, part):
    key = jax.random.fold_in(key, 7)
    first_key, second_key = jax.random.split(key)
    half_count = BLOCKS // 2
    lower_half = jax.random.permutation(first_key, half_count).astype(jnp.int32)
    swapped = jax.random.randint(second_key, (half_count,), 0, 2, dtype=jnp.int32)
    upper_half = BLOCKS - 1 - lower_half
    leading = jnp.where(swapped == 1, upper_half, lower_half)
    trailing = jnp.where(swapped == 1, lower_half, upper_half)
    return jnp.stack([leading, trailing], axis=1).reshape(BLOCKS).astype(jnp.int32)


def shard_levels(rng, extent, pieces, least, top_value):
    def one(dim, shards_of):
        steps = jax.random.uniform(jax.random.fold_in(jax.random.fold_in(rng, 6), dim), (shards_of,), jnp.float32, least / len(pieces), top_value / len(pieces))
        return jnp.repeat(jnp.exp(steps), extent[dim] // shards_of).reshape((-1,) + (1,) * (len(extent) - dim - 1))

    gain = one(*pieces[0])
    for cut in pieces[1:]:
        gain = gain * one(*cut)
    return gain


def normal_values(stream_key, dims, width, bound, cuts=(), kind=jnp.bfloat16):
    level = shard_levels(stream_key, dims, cuts, -0.22, 0.18) if cuts else 1.0
    entries = jax.random.normal(stream_key, dims, jnp.float32) * width * level
    return jnp.minimum(jnp.maximum(entries, -bound), bound).astype(kind)


def setup_inputs(seed: int = 0) -> dict:
    key_of = jax.random.split(jax.random.key(seed), 17)
    return {
        "tokens": normal_values(key_of[0], (SEQS_ALL, SEQ_LEN, D), 1.0, 6.0, ((0, 2), (1, 64))),
        "attn_gain": jnp.clip(1.0 + 0.18 * jax.random.normal(key_of[1], (D,), jnp.float32), 0.099609375, 1.8984375).astype(jnp.bfloat16),
        "attn_shift": normal_values(key_of[2], (D,), 0.3, 1.75, ((0, 2),)),
        "input_weight": normal_values(key_of[3], (D, 3 * D), D ** -0.5, 0.21875, ((0, 2),)),
        "query_bias": normal_values(key_of[4], (D,), 0.5, 3.0, ((0, 2),)),
        "value_bias": normal_values(key_of[5], (D,), 0.5, 3.0, ((0, 2),)),
        "output_weight": normal_values(key_of[6], (D, D), (max(1, 4 * D // SEQ_LEN)) ** -0.5, 6.0, ((0, 2),)),
        "output_bias": normal_values(key_of[7], (D,), 0.3, 1.75, ((0, 2),)),
        "mlp_gain": jnp.clip(1.0 + 0.18 * jax.random.normal(key_of[8], (D,), jnp.float32), 0.099609375, 1.8984375).astype(jnp.bfloat16),
        "mlp_shift": normal_values(key_of[9], (D,), 0.3, 1.75, ((0, 2),)),
        "hidden_weight": normal_values(key_of[10], (D, FF), D ** -0.5, 0.21875, ((0, 2),)),
        "hidden_bias": normal_values(key_of[11], (FF,), 0.5, 3.0, ((0, 2),)),
        "return_weight": normal_values(key_of[12], (FF, D), FF ** -0.5, 0.109375, ((0, 2),)),
        "return_bias": normal_values(key_of[13], (D,), 0.3, 1.75, ((0, 2),)),
        "block_order": draw_block_order(jax.random.fold_in(key_of[16], 71), 0),
        "cotangent": normal_values(key_of[15], (SEQS_ALL, SEQ_LEN, D), 1.0, 6.0, ((0, 2), (1, 64))),
    }


@jax.custom_vjp
def low(v):
    return lax.optimization_barrier(v.astype(jnp.bfloat16)).astype(jnp.float32)

@jax.custom_vjp
def low_back(v):
    return v

def low_keep(v):
    return (low(v), None)

def low_pass(kept, grad):
    return (grad,)

def back_keep(v):
    return (v, None)

def back_low(kept, grad):
    return (low(grad),)
low.defvjp(low_keep, low_pass)
low_back.defvjp(back_keep, back_low)

def layer_norm(values, scale_vec, shift_vec):
    center = values - lax.optimization_barrier(jnp.mean(values, -1, keepdims=True))
    spread = lax.optimization_barrier(jnp.mean(center * center, -1, keepdims=True))
    return center * lax.rsqrt(spread + 1e-05) * scale_vec + shift_vec

def attention(queries, keys, values, positions):
    length = queries.shape[0]
    qblock = 512 if length % 512 == 0 else length
    query_heads = queries.reshape(length // qblock, qblock, H, HEAD_DIM)
    query_pos = positions.reshape(length // qblock, qblock)
    key_heads = keys.reshape(length, H, HEAD_DIM)
    value_heads = values.reshape(length, H, HEAD_DIM)

    def one_block(inputs):
        block_queries, block_pos = inputs
        scores = jnp.einsum('qhd,khd->hqk', block_queries, key_heads, precision=lax.Precision.HIGHEST) * 0.125
        scores = low_back(scores)
        allowed = positions[None, None, :] <= block_pos[None, :, None]
        scores = jnp.where(allowed, scores, -1e+30)
        probs = jax.nn.softmax(scores, axis=-1)
        mixed = jnp.einsum('hqk,khd->qhd', low(probs), value_heads, precision=lax.Precision.HIGHEST)
        return mixed.reshape(qblock, H * HEAD_DIM)
    return lax.map(jax.checkpoint(one_block), (query_heads, query_pos)).reshape(length, H * HEAD_DIM)

def forward(tokens_row, params, positions):
    attn_gain, attn_shift, input_weight, query_bias, value_bias, output_weight, output_bias, mlp_gain, mlp_shift, hidden_weight, hidden_bias, return_weight, return_bias = params
    highest = lax.Precision.HIGHEST
    norm_one = low(layer_norm(tokens_row, attn_gain, attn_shift))
    projected = jnp.dot(norm_one, input_weight, precision=highest)
    queries = low_back(low(projected[:, :D] + query_bias))
    keys = low_back(low(projected[:, D:2 * D]))
    values = low_back(low(projected[:, 2 * D:] + value_bias))
    attended = low_back(low(attention(queries, keys, values, positions)))
    branch = low_back(jnp.dot(attended, output_weight, precision=highest) + output_bias)
    middle = tokens_row + branch
    norm_two = low(layer_norm(middle, mlp_gain, mlp_shift))
    pre_act = low_back(jnp.dot(norm_two, hidden_weight, precision=highest) + hidden_bias)
    acted = low(jax.nn.gelu(pre_act, approximate=True))
    return middle + jnp.dot(acted, return_weight, precision=highest) + return_bias

def reference(tokens, attn_gain, attn_shift, input_weight, query_bias, value_bias, output_weight, output_bias, mlp_gain, mlp_shift, hidden_weight, hidden_bias, return_weight, return_bias, block_order, cotangent):
    params = tuple((p.astype(jnp.float32) for p in (attn_gain, attn_shift, input_weight, query_bias, value_bias, output_weight, output_bias, mlp_gain, mlp_shift, hidden_weight, hidden_bias, return_weight, return_bias)))
    positions = (block_order[:, None] * BLK + jnp.arange(BLK, dtype=jnp.int32)[None, :]).reshape(-1).astype(jnp.int32)

    def one_sequence(totals, inputs):
        tokens_row, grad_row = inputs
        result, pull = jax.vjp(lambda rows_in, weights_in: forward(rows_in, weights_in, positions), tokens_row.astype(jnp.float32), params)
        grad_tokens, grad_params = pull(grad_row.astype(jnp.float32))
        totals = jax.tree.map(jnp.add, totals, grad_params)
        return (totals, (result.astype(jnp.bfloat16), grad_tokens.astype(jnp.bfloat16)))
    zeros = jax.tree.map(jnp.zeros_like, params)
    grads, (outputs, input_grads) = lax.scan(one_sequence, zeros, (tokens, cotangent))
    return (outputs, input_grads, grads[0], grads[1], grads[2], grads[3], grads[4], grads[5], grads[6], grads[7], grads[8], grads[9], grads[10], grads[11], grads[12])
```

```python
import jax
import jax.numpy as jnp
from jax import lax
from jax.experimental import pallas as pl
from jax.experimental.pallas import tpu as pltpu
from jax.sharding import Mesh
from jax.sharding import PartitionSpec as P

HEAD = 64
BLK = 64
TILE = 256
GROUP = TILE // BLK
HEADS = 3
WIDTH = HEADS * HEAD
PACK = 256
NEG = -1e30
CTX = ("zl", "x", "y", "co")

f32 = jnp.float32
bf16 = jnp.bfloat16


def nn(a, b):
    return lax.dot_general(a, b, (((1,), (0,)), ((), ())), preferred_element_type=f32)


def nt(a, b):
    return lax.dot_general(a, b, (((1,), (1,)), ((), ())), preferred_element_type=f32)


def tn(a, b):
    return lax.dot_general(a, b, (((0,), (0,)), ((), ())), preferred_element_type=f32)


def eye_low():
    r = lax.broadcasted_iota(jnp.int32, (HEAD, HEAD), 0)
    c = lax.broadcasted_iota(jnp.int32, (HEAD, HEAD), 1)
    return jnp.where(r == c, 1.0, 0.0).astype(bf16)


def rows_of(start, size):
    return pl.ds(pl.multiple_of(start * size, size), size)


def tile_positions(blocks, tile, axis, shape):
    r = lax.broadcasted_iota(jnp.int32, shape, axis)
    base = jnp.full(shape, blocks[tile * GROUP], jnp.int32)
    for a in range(1, GROUP):
        base = jnp.where(r >= a * BLK, blocks[tile * GROUP + a], base)
    return base * BLK + (r & (BLK - 1))


LOG2E = 1.4426950408889634
LN2 = 0.6931471805599453


def two_terms(values):
    high = values.astype(bf16)
    low = (values - high.astype(f32)).astype(bf16)
    return jnp.concatenate([high, low], axis=0)


def sort_rows(count, perm, src, parts):
    def one(b, _):
        rows = src[rows_of(perm[b], BLK), :]
        for dst, col, scale in parts:
            for h in range(HEADS):
                piece = rows[:, col + h * HEAD : col + (h + 1) * HEAD]
                if scale != 1.0:
                    piece = (piece.astype(f32) * scale).astype(bf16)
                wide = dst.shape[2] // HEAD
                if wide > 1:
                    piece = jnp.concatenate([piece] * wide, axis=1)
                dst[h, rows_of(b, BLK), :] = piece
        return 0

    lax.fori_loop(0, count, one, 0, unroll=4)


def transpose_heads(src, dst, tiles):
    eye = eye_low()

    def one(t, _):
        for h in range(HEADS):
            dst[h, :, rows_of(t, TILE)] = nt(eye, src[h, rows_of(t, TILE), :]).astype(bf16)
        return 0

    lax.fori_loop(0, tiles, one, 0)


def forward_kernel(
    qperm, qblk, kperm, kblk, last, full, q_ref, kv_ref, out_ref, qs, ks, vs, vt, m, l, acc, pack
):
    q_blocks = q_ref.shape[0] // BLK
    k_blocks = kv_ref.shape[0] // BLK
    sort_rows(q_blocks, qperm, q_ref, [(qs, 0, 0.125)])
    sort_rows(k_blocks, kperm, kv_ref, [(ks, 0, 1.0), (vs, WIDTH, 1.0)])
    transpose_heads(vs, vt, k_blocks // GROUP)
    pack[...] = jnp.zeros_like(pack)
    eye = eye_low()

    def q_tile(i, _):
        m[...] = jnp.full_like(m, NEG)
        l[...] = jnp.zeros_like(l)
        acc[...] = jnp.zeros_like(acc)
        qpos = tile_positions(qblk, i, 1, (1, TILE))
        qt = [two_terms(nt(eye, qs[h, rows_of(i, TILE), :]) * LOG2E) for h in range(HEADS)]

        def step(j, masked):
            tiles = [j * 2, j * 2 + 1]
            pairs = [(h, t) for h in range(HEADS) for t in range(2)]
            s = {
                (h, t): nn(ks[h, rows_of(tiles[t], TILE), :], qt[h]) for h, t in pairs
            }
            if masked:
                for t in range(2):
                    allowed = tile_positions(kblk, tiles[t], 0, (TILE, TILE)) <= qpos
                    for h in range(HEADS):
                        s[h, t] = jnp.where(allowed, s[h, t], NEG)
            old = [m[h] for h in range(HEADS)]
            new = [
                jnp.maximum(old[h], jnp.max(jnp.maximum(s[h, 0], s[h, 1]), 0, keepdims=True))
                for h in range(HEADS)
            ]
            p = {(h, t): jnp.exp2(s[h, t] - new[h]) for h, t in pairs}
            part = [
                nn(vt[h, :, rows_of(tiles[0], TILE)], p[h, 0].astype(bf16))
                + nn(vt[h, :, rows_of(tiles[1], TILE)], p[h, 1].astype(bf16))
                for h in range(HEADS)
            ]
            for h in range(HEADS):
                keep = jnp.exp2(old[h] - new[h])
                m[h] = new[h]
                l[h] = l[h] * keep + jnp.sum(p[h, 0] + p[h, 1], 0, keepdims=True)
                acc[h] = acc[h] * keep + part[h]

        def open_step(j, _):
            step(j, False)
            return 0

        def edge_step(j, _):
            step(j, True)
            return 0

        lax.fori_loop(0, full[i] // 2, open_step, 0)
        lax.fori_loop(full[i] // 2, (last[i] + 1) // 2, edge_step, 0)
        stats = []
        for h in range(HEADS):
            total = l[h]
            total = jnp.where(total > 0.0, total, 1.0)
            pack[h * HEAD : (h + 1) * HEAD, :] = acc[h] * (1.0 / total)
            stats.append(m[h] * LN2 + jnp.log(total))
        stat = jnp.concatenate(stats + [jnp.zeros((8 - HEADS, TILE), f32)], axis=0)
        for part in range(3):
            low = stat.astype(bf16).astype(f32)
            pack[WIDTH + part * 8 : WIDTH + part * 8 + 8, :] = low
            stat = stat - low
        rows = pack[...].T.astype(bf16)
        for a in range(GROUP):
            out_ref[rows_of(qperm[i * GROUP + a], BLK), :] = rows[a * BLK : (a + 1) * BLK, :]
        return 0

    lax.fori_loop(0, q_blocks // GROUP, q_tile, 0)


def backward_kernel(
    qperm, qblk, kperm, kblk, last, full, q_ref, kv_ref, do_ref, dq_ref, dkv_ref,
    qs, ks, vs, kt, dos, stat, dk, dv, acc, pack,
):
    q_blocks = q_ref.shape[0] // BLK
    k_blocks = kv_ref.shape[0] // BLK
    sort_rows(q_blocks, qperm, q_ref, [(qs, 0, 0.125)])
    sort_rows(k_blocks, kperm, kv_ref, [(ks, 0, 1.0), (vs, WIDTH, 1.0)])
    sort_rows(q_blocks, qperm, do_ref, [(dos, 0, 1.0)])

    def sort_stats(b, _):
        stat[rows_of(b, BLK), :] = do_ref[rows_of(qperm[b], BLK), 128:].astype(f32)
        return 0

    lax.fori_loop(0, q_blocks, sort_stats, 0)
    eye = eye_low()
    keys = ks.shape[1]
    lane = lax.broadcasted_iota(jnp.int32, (keys, HEAD), 1)
    ones = jnp.where(lane < 3, 1.0, 0.0).astype(bf16)
    for h in range(HEADS):
        ks[h, :, 2 * HEAD :] = ones
        vs[h, :, HEAD:] = ones

    def transpose_keys(t, _):
        for h in range(HEADS):
            kt[h, :, rows_of(t, TILE)] = nt(eye, ks[h, rows_of(t, TILE), :HEAD]).astype(bf16)
        return 0

    lax.fori_loop(0, k_blocks // GROUP, transpose_keys, 0)
    dk[...] = jnp.zeros_like(dk)
    dv[...] = jnp.zeros_like(dv)
    pack[...] = jnp.zeros_like(pack)

    def less(row):
        rows = []
        for _ in range(3):
            low = row.astype(bf16).astype(f32)
            rows.append(-low)
            row = row - low
        rows.append(jnp.zeros((5, row.shape[1]), f32))
        rows.append(jnp.zeros((HEAD - 8, row.shape[1]), f32))
        return jnp.concatenate(rows, axis=0).astype(bf16)

    def q_tile(i, _):
        acc[...] = jnp.zeros_like(acc)
        qpos = tile_positions(qblk, i, 1, (1, TILE))
        columns = stat[rows_of(i, TILE), :].T
        first = WIDTH - 128
        lse = columns[first : first + 8] + columns[first + 8 : first + 16] + columns[first + 16 : first + 24]
        first = first + 24
        delta = columns[first : first + 8] + columns[first + 8 : first + 16] + columns[first + 16 : first + 24]
        qr = rows_of(i, TILE)
        each = range(HEADS)
        qt = [
            jnp.concatenate([
                two_terms(nt(eye, qs[h, qr, :]) * LOG2E), less(lse[h : h + 1] * LOG2E)
            ], axis=0)
            for h in each
        ]
        dot = [
            jnp.concatenate([nt(eye, dos[h, qr, :]).astype(bf16), less(delta[h : h + 1])], axis=0)
            for h in each
        ]

        def step(j, masked):
            kr = rows_of(j, TILE)
            s = [nn(ks[h, kr, :], qt[h]) for h in each]
            dp = [nn(vs[h, kr, :], dot[h]) for h in each]
            p = [jnp.exp2(s[h]) for h in each]
            if masked:
                kpos = tile_positions(kblk, j, 0, (TILE, TILE))
                p = [jnp.where(kpos <= qpos, p[h], 0.0) for h in each]
            low = [p[h].astype(bf16) for h in each]
            ds = [(p[h] * dp[h]).astype(bf16) for h in each]
            dv_part = [nn(low[h], dos[h, qr, :]) for h in each]
            dk_part = [nn(ds[h], qs[h, qr, :]) for h in each]
            dq_part = [nn(kt[h, :, kr], ds[h]) for h in each]
            for h in each:
                dv[h, kr, :] += dv_part[h]
                dk[h, kr, :] += dk_part[h]
                acc[h] += dq_part[h]

        def open_step(j, _):
            step(j, False)
            return 0

        def edge_step(j, _):
            step(j, True)
            return 0

        lax.fori_loop(0, full[i], open_step, 0)
        lax.fori_loop(full[i], last[i], edge_step, 0)
        for h in range(HEADS):
            pack[h * HEAD : (h + 1) * HEAD, :] = acc[h] * 0.125
        rows = pack[...].T.astype(bf16)
        for a in range(GROUP):
            dq_ref[rows_of(qperm[i * GROUP + a], BLK), :] = rows[a * BLK : (a + 1) * BLK, :WIDTH]
        return 0

    lax.fori_loop(0, q_blocks // GROUP, q_tile, 0)

    def put(b, _):
        r = rows_of(b, BLK)
        pieces = [dk[h, r, :] for h in range(HEADS)] + [dv[h, r, :] for h in range(HEADS)]
        dkv_ref[rows_of(kperm[b], BLK), :] = jnp.concatenate(pieces, axis=1).astype(bf16)
        return 0

    lax.fori_loop(0, k_blocks, put, 0)


def spread_stats(rows, groups):
    lane = lax.broadcasted_iota(jnp.int32, (rows, HEAD), 1)
    out = jnp.zeros((rows, HEAD), f32)
    for g, values in enumerate(groups):
        for h, value in enumerate(values):
            for term in range(3):
                piece = value.astype(bf16).astype(f32)
                out = jnp.where(lane == g * 24 + term * 8 + h, piece, out)
                value = value - piece
    return out


def merge_kernel(p0, p1, p2, p3, w_ref, att_ref, low_ref, stat_ref, branch_ref):
    parts = [p[...].astype(f32) for p in (p0, p1, p2, p3)]
    rows = p0.shape[0]
    lane = lax.broadcasted_iota(jnp.int32, (rows, PACK), 1)
    shares = [None] * 4
    logs = jnp.zeros((rows, 128), f32)
    for h in range(HEADS):
        c = WIDTH + h
        lse = [p[:, c : c + 1] + p[:, c + 8 : c + 9] + p[:, c + 16 : c + 17] for p in parts]
        top = jnp.maximum(jnp.maximum(lse[0], lse[1]), jnp.maximum(lse[2], lse[3]))
        w = [jnp.exp(v - top) for v in lse]
        total = (w[0] + w[1]) + (w[2] + w[3])
        scale = 1.0 / total
        for n in range(4):
            share = jnp.broadcast_to(w[n] * scale, (rows, PACK))
            shares[n] = share if h == 0 else jnp.where(lane >= h * HEAD, share, shares[n])
        logs = jnp.where(lane[:, :128] == h, top + jnp.log(total), logs)
    mixed = parts[0] * shares[0]
    for n in range(1, 4):
        mixed = mixed + parts[n] * shares[n]
    mixed = mixed[:, :WIDTH]
    low = mixed.astype(bf16)
    att_ref[...] = mixed
    low_ref[...] = low
    stat_ref[...] = logs
    branch_ref[...] = nn(low, w_ref[...]).astype(bf16)


def merge(parts, weight_out):
    rows = parts[0].shape[0]
    vmem = pl.BlockSpec(memory_space=pltpu.VMEM)
    return pl.pallas_call(
        merge_kernel,
        name="merge_partials",
        out_shape=(
            jax.ShapeDtypeStruct((rows, WIDTH), f32),
            jax.ShapeDtypeStruct((rows, WIDTH), bf16),
            jax.ShapeDtypeStruct((rows, 128), f32),
            jax.ShapeDtypeStruct((rows, weight_out.shape[1]), bf16),
        ),
        in_specs=[vmem] * 5,
        out_specs=(vmem,) * 4,
        compiler_params=pltpu.CompilerParams(vmem_limit_bytes=32 * 2**20),
        cost_estimate=pl.CostEstimate(
            flops=2 * rows * WIDTH * weight_out.shape[1],
            bytes_accessed=2 * rows * (4 * PACK + 3 * WIDTH + 1024), transcendentals=rows * 16,
        ),
    )(*parts, weight_out)


def do_kernel(g_ref, w_ref, att_ref, stat_ref, out_ref):
    rows = g_ref.shape[0]
    low = nt(g_ref[...], w_ref[...]).astype(bf16)
    prod = low.astype(f32) * att_ref[...]
    logs = stat_ref[...]
    each = range(HEADS)
    deltas = [
        jnp.sum(prod[:, h * HEAD : (h + 1) * HEAD], -1, keepdims=True) for h in each
    ]
    extra = spread_stats(rows, [[logs[:, h : h + 1] for h in each], deltas])
    out_ref[...] = jnp.concatenate([low, extra.astype(bf16)], axis=1)


def grad_attended_packed(grad_branch, weight_out, attended, stats):
    rows = grad_branch.shape[0]
    vmem = pl.BlockSpec(memory_space=pltpu.VMEM)
    return pl.pallas_call(
        do_kernel,
        name="grad_attended",
        out_shape=jax.ShapeDtypeStruct((rows, PACK), bf16),
        in_specs=[vmem] * 4,
        out_specs=vmem,
        compiler_params=pltpu.CompilerParams(vmem_limit_bytes=32 * 2**20),
        cost_estimate=pl.CostEstimate(
            flops=2 * rows * WIDTH * weight_out.shape[1],
            bytes_accessed=2 * rows * (1024 + 4 * WIDTH), transcendentals=0,
        ),
    )(grad_branch, weight_out, attended, stats)


VMEM = pl.BlockSpec(memory_space=pltpu.VMEM)
SMEM = pl.BlockSpec(memory_space=pltpu.SMEM)
PART = 24
VEC = 6


def vector_block(row, half, first):
    blocks = []
    for f in range(2):
        cut = [
            row[:, f * half + r * HEAD : f * half + (r + 1) * HEAD] for r in range(VEC)
        ]
        before = [jnp.zeros((first, HEAD), f32)] if first else []
        after = [jnp.zeros((PART - VEC - first, HEAD), f32)]
        blocks.append(jnp.concatenate(before + cut + after, axis=0))
    return blocks


def keep_and_give(core, n, first, second, keep_ref, give_ref):
    mine = core == 0
    keep_ref[n] = jnp.where(mine, first, second).astype(bf16)
    give_ref[n] = jnp.where(mine, second, first).astype(bf16)


def mlp_grads_kernel(core, acted, cot, norm, grad, keep_ref, give_ref):
    hid = tn(norm[...], grad[...])
    ret = tn(acted[...], cot[...])
    for n in range(16):
        pair = []
        for c in range(2):
            r = n * 2 * PART + c * PART
            pair.append(jnp.concatenate([hid[r : r + PART], ret[r : r + PART]], axis=0))
        keep_and_give(core[0], n, pair[0], pair[1], keep_ref, give_ref)


def mlp_grads(core, acted, cot, norm, grad):
    width = norm.shape[1]
    chunk = jax.ShapeDtypeStruct((16, 2 * PART, width), bf16)
    return pl.pallas_call(
        mlp_grads_kernel,
        name="mlp_weight_grads",
        out_shape=(chunk, chunk),
        in_specs=[SMEM] + [VMEM] * 4,
        out_specs=(VMEM, VMEM),
        compiler_params=pltpu.CompilerParams(vmem_limit_bytes=40 * 2**20),
        cost_estimate=pl.CostEstimate(
            flops=4 * norm.shape[0] * width * width, bytes_accessed=6_000_000, transcendentals=0
        ),
    )(core, acted, cot, norm, grad)


def mid_kernel(yi, low, branch, cot, gn, xhat, gpre, out_ref):
    rows, width = cot.shape
    half = width // 2
    w_out = tn(low[...], branch[...])
    own = branch[...][:rows].astype(f32)
    vectors = [
        jnp.sum(cot[...].astype(f32), 0, keepdims=True),
        jnp.sum(gn[...] * xhat[...], 0, keepdims=True),
        jnp.sum(gn[...], 0, keepdims=True),
        jnp.sum(own, 0, keepdims=True),
        jnp.sum(gpre[...].astype(f32), 0, keepdims=True),
    ]
    blocks = [vector_block(v, half, 8) for v in vectors]
    empty = jnp.zeros((PART, HEAD), f32)
    for f in range(2):
        mine = jnp.where(yi[0] // 2 == f, 1.0, 0.0).astype(f32)
        for n in range(8):
            for core in range(2):
                k = n * 2 + core
                w = w_out[n * PART : (n + 1) * PART, core * half : (core + 1) * half] * mine
                v = blocks[k][f] if k < len(blocks) else empty
                out_ref[core, f * 8 + n] = jnp.concatenate([w, v], axis=1).astype(bf16)


def mid_chunks(yi, low, branch, cot, gn, xhat, gpre):
    width = cot.shape[1]
    return pl.pallas_call(
        mid_kernel,
        name="mid_gradients",
        out_shape=jax.ShapeDtypeStruct((2, 16, PART, width // 2 + HEAD), bf16),
        in_specs=[SMEM] + [VMEM] * 6,
        out_specs=VMEM,
        compiler_params=pltpu.CompilerParams(vmem_limit_bytes=40 * 2**20),
        cost_estimate=pl.CostEstimate(
            flops=2 * low.shape[0] * low.shape[1] * width, bytes_accessed=4_000_000,
            transcendentals=0,
        ),
    )(yi, low, branch, cot, gn, xhat, gpre)


def late_kernel(
    where, q0, q1, q2, q3, v0, v1, norm, xhat, w_in, mid, keep_ref, give_ref, part_ref
):
    width = norm.shape[1]
    half = width // 2
    dq = add_up([r[...] for r in (q0, q1, q2, q3)])
    dkv = add_up([r[...] for r in (v0, v1)])
    grad = jnp.concatenate([dq, dkv], axis=1).astype(bf16)
    part = nt(grad, w_in[...])
    part_ref[...] = part.astype(bf16)
    w = tn(norm[...], grad)
    sums = jnp.sum(grad.astype(f32), 0, keepdims=True)
    lane = lax.broadcasted_iota(jnp.int32, (1, width), 1)
    inside = (lane >= where[0] * WIDTH) & (lane < (where[0] + 1) * WIDTH)

    def spread(piece):
        return jnp.where(inside, jnp.concatenate([piece] * 4, axis=1), 0.0)

    vectors = [
        jnp.sum(part * xhat[...], 0, keepdims=True),
        jnp.sum(part, 0, keepdims=True),
        spread(sums[:, :WIDTH]),
        spread(sums[:, 2 * WIDTH :]),
    ]
    blocks = [vector_block(v, half, 0) for v in vectors]
    for n in range(16):
        pair = []
        for c in range(2):
            k = (n % 8) * 2 + c
            r = n * 2 * PART + c * PART
            early = mid[c, n].astype(f32)
            tail = early[:, half:]
            if k < len(blocks):
                tail = tail + blocks[k][n // 8]
            pair.append(jnp.concatenate([w[r : r + PART], early[:, :half], tail], axis=1))
        keep_and_give(where[1], n, pair[0], pair[1], keep_ref, give_ref)


def late_chunks(where, dq_terms, dkv_terms, norm, xhat, w_in, mid):
    rows, width = norm.shape
    chunk = jax.ShapeDtypeStruct((16, PART, 3 * WIDTH + mid.shape[3]), bf16)
    return pl.pallas_call(
        late_kernel,
        name="late_gradients",
        out_shape=(chunk, chunk, jax.ShapeDtypeStruct((rows, width), bf16)),
        in_specs=[SMEM] + [VMEM] * 10,
        out_specs=(VMEM, VMEM, VMEM),
        compiler_params=pltpu.CompilerParams(vmem_limit_bytes=48 * 2**20),
        cost_estimate=pl.CostEstimate(
            flops=4 * rows * width * 3 * WIDTH, bytes_accessed=8_000_000, transcendentals=0
        ),
    )(where, *dq_terms, *dkv_terms, norm, xhat, w_in, mid)


def sum_wide_kernel(got, out_ref):
    total = got[0].astype(f32)
    for n in range(1, got.shape[0]):
        total = total + got[n].astype(f32)
    row = total.astype(bf16)
    for n in range(out_ref.shape[0]):
        out_ref[n] = row


def sum_wide(got):
    return pl.pallas_call(
        sum_wide_kernel,
        name="sum_chunks",
        out_shape=jax.ShapeDtypeStruct((32,) + got.shape[1:], bf16),
        in_specs=[VMEM],
        out_specs=VMEM,
        compiler_params=pltpu.CompilerParams(vmem_limit_bytes=32 * 2**20),
        cost_estimate=pl.CostEstimate(flops=0, bytes_accessed=4_000_000, transcendentals=0),
    )(got)


def place_early_kernel(where, mine, other, hid_ref, ret_ref):
    first = where[0] == 0
    half = mine.shape[3] // 2
    for core in range(2):
        rows = slice(core * PART, core * PART + PART)
        take = first if core == 0 else jnp.logical_not(first)
        for y in range(4):
            block = jnp.where(take, mine[0, y], other[0, y]).astype(f32)
            for f in range(2):
                col = f * 4 * half + y * half
                hid_ref[rows, col : col + half] = block[:PART, f * half : (f + 1) * half]
            ret_ref[y, rows, :] = block[PART:]


def place_early(where, mine, other):
    n, width = mine.shape[0], mine.shape[3]
    block = pl.BlockSpec((1,) + mine.shape[1:], lambda i: (i, 0, 0, 0))
    hid, ret = pl.pallas_call(
        place_early_kernel,
        name="place_early_gradients",
        grid=(n,),
        out_shape=(
            jax.ShapeDtypeStruct((n * 2 * PART, 4 * width), f32),
            jax.ShapeDtypeStruct((4, n * 2 * PART, width), f32),
        ),
        in_specs=[SMEM, block, block],
        out_specs=(
            pl.BlockSpec((2 * PART, 4 * width), lambda i: (i, 0)),
            pl.BlockSpec((4, 2 * PART, width), lambda i: (0, i, 0)),
        ),
        compiler_params=pltpu.CompilerParams(vmem_limit_bytes=32 * 2**20),
        cost_estimate=pl.CostEstimate(flops=0, bytes_accessed=18_000_000, transcendentals=0),
    )(where, mine, other)
    return hid, ret.reshape(-1, width)


def place_late_kernel(where, data, *refs):
    in_ref, out_ref, vec_ref = refs[-3:]
    base = where[1] * 2
    half = out_ref.shape[3]
    start = 3 * WIDTH + half
    for n in range(data.shape[0]):
        block = [data[n, y].astype(f32) for y in range(4)]
        pieces = [block[y][:, t * WIDTH : (t + 1) * WIDTH] for t in range(3) for y in range(4)]
        in_ref[n, 0] = jnp.concatenate(pieces, axis=1)
        for y in range(2):
            out_ref[y, n] = data[n, base + y].astype(f32)[:, 3 * WIDTH : start]

        def vector(rows_in, at):
            cut = [rows_in[at + r : at + r + 1, start:] for r in range(VEC)]
            return jnp.concatenate(cut, axis=1)

        total = (block[0] + block[1]) + (block[2] + block[3])
        late, mid = vector(total, 0), vector(total, 8)
        vec_ref[n, 0] = jnp.concatenate(
            [late, mid, late, mid] + [vector(block[y], 8) for y in range(4)], axis=0)


def place_late(where, data, filled=()):
    n = data.shape[0]
    some = n // 2
    half = data.shape[3] - 3 * WIDTH - HEAD
    return pl.pallas_call(
        place_late_kernel,
        name="place_late_gradients",
        grid_spec=pltpu.PrefetchScalarGridSpec(
            num_scalar_prefetch=1,
            grid=(n // some,),
            in_specs=[pl.BlockSpec((some,) + data.shape[1:], lambda i, w: (i, 0, 0, 0))]
            + [pl.BlockSpec(memory_space=pl.ANY)] * len(filled),
            out_specs=(
                pl.BlockSpec((some, 1, PART, 12 * WIDTH), lambda i, w: (i, w[0], 0, 0)),
                pl.BlockSpec((2, some, PART, half), lambda i, w: (0, i, 0, w[0])),
                pl.BlockSpec((some, 1, 8, half), lambda i, w: (i, w[0], 0, 0)),
            ),
        ),
        out_shape=(
            jax.ShapeDtypeStruct((n, 2, PART, 12 * WIDTH), f32),
            jax.ShapeDtypeStruct((2, n, PART, 2 * half), f32),
            jax.ShapeDtypeStruct((n, 2, 8, half), f32),
        ),
        input_output_aliases={2 + k: k for k in range(len(filled))},
        compiler_params=pltpu.CompilerParams(vmem_limit_bytes=32 * 2**20),
        cost_estimate=pl.CostEstimate(flops=0, bytes_accessed=4_000_000, transcendentals=0),
    )(where, data, *filled)


def attention_forward(plan, q, kv):
    rows, keys = q.shape[0], kv.shape[0]
    smem = pl.BlockSpec(memory_space=pltpu.SMEM)
    vmem = pl.BlockSpec(memory_space=pltpu.VMEM)
    return pl.pallas_call(
        forward_kernel,
        name="attention_forward",
        out_shape=jax.ShapeDtypeStruct((rows, PACK), bf16),
        in_specs=[smem] * 6 + [vmem] * 2,
        out_specs=vmem,
        scratch_shapes=[
            pltpu.VMEM((HEADS, rows, HEAD), bf16),
            pltpu.VMEM((HEADS, keys, 2 * HEAD), bf16),
            pltpu.VMEM((HEADS, keys, HEAD), bf16),
            pltpu.VMEM((HEADS, HEAD, keys), bf16),
            pltpu.VMEM((HEADS, 1, TILE), f32),
            pltpu.VMEM((HEADS, 1, TILE), f32),
            pltpu.VMEM((HEADS, HEAD, TILE), f32),
            pltpu.VMEM((PACK, TILE), f32),
        ],
        compiler_params=pltpu.CompilerParams(vmem_limit_bytes=48 * 2**20),
        cost_estimate=pl.CostEstimate(
            flops=16 * 2 * rows * keys * WIDTH,
            bytes_accessed=2 * (rows * WIDTH + keys * 2 * WIDTH + rows * PACK),
            transcendentals=rows * keys * HEADS // 2,
        ),
    )(*plan, q, kv)


def attention_backward(plan, q, kv, do):
    rows, keys = q.shape[0], kv.shape[0]
    smem = pl.BlockSpec(memory_space=pltpu.SMEM)
    vmem = pl.BlockSpec(memory_space=pltpu.VMEM)
    return pl.pallas_call(
        backward_kernel,
        name="attention_backward",
        out_shape=(
            jax.ShapeDtypeStruct((rows, WIDTH), bf16),
            jax.ShapeDtypeStruct((keys, 2 * WIDTH), bf16),
        ),
        in_specs=[smem] * 6 + [vmem] * 3,
        out_specs=(vmem, vmem),
        scratch_shapes=[
            pltpu.VMEM((HEADS, rows, HEAD), bf16),
            pltpu.VMEM((HEADS, keys, 3 * HEAD), bf16),
            pltpu.VMEM((HEADS, keys, 2 * HEAD), bf16),
            pltpu.VMEM((HEADS, HEAD, keys), bf16),
            pltpu.VMEM((HEADS, rows, HEAD), bf16),
            pltpu.VMEM((rows, 128), f32),
            pltpu.VMEM((HEADS, keys, HEAD), f32),
            pltpu.VMEM((HEADS, keys, HEAD), f32),
            pltpu.VMEM((HEADS, HEAD, TILE), f32),
            pltpu.VMEM((PACK, TILE), f32),
        ],
        compiler_params=pltpu.CompilerParams(vmem_limit_bytes=48 * 2**20),
        cost_estimate=pl.CostEstimate(
            flops=24 * 2 * rows * keys * WIDTH,
            bytes_accessed=2 * (rows * 4 * WIDTH + keys * 4 * WIDTH),
            transcendentals=rows * keys * HEADS // 2,
        ),
    )(*plan, q, kv, do)


def sorted_blocks(blocks):
    n = blocks.shape[0]
    ids = jnp.arange(n, dtype=jnp.int32)
    rank = jnp.sum((blocks[None, :] < blocks[:, None]).astype(jnp.int32), 1)
    hit = (rank[None, :] == ids[:, None]).astype(jnp.int32)
    return jnp.sum(hit * ids[None, :], 1), jnp.sum(hit * blocks[None, :], 1)


def attention_plan(q_blocks, k_blocks):
    qperm, qblk = sorted_blocks(q_blocks)
    kperm, kblk = sorted_blocks(k_blocks)
    top = qblk[GROUP - 1 :: GROUP]
    low = qblk[::GROUP]
    seen = jnp.sum((kblk[None, :] <= top[:, None]).astype(jnp.int32), 1)
    below = jnp.sum((kblk[None, :] < low[:, None]).astype(jnp.int32), 1)
    last = (seen + GROUP - 1) // GROUP
    full = below // GROUP
    return qperm, qblk, kperm, kblk, last, full


def shift(rows, axis, s):
    return lax.ppermute(rows, axis, [(i, (i + s) % 4) for i in range(4)])


def swap(rows, axis, s, count):
    return lax.ppermute(rows, axis, [(i, i ^ s) for i in range(count)])


def gather_shifts(rows, axis):
    return jnp.concatenate([rows] + [shift(rows, axis, s) for s in range(1, 4)], axis=0)


def gather_swaps(rows):
    return jnp.concatenate(
        [rows] + [swap(rows, ("zl", "co"), mask, 4) for mask in (2, 1, 3)], axis=0)


def back_shifts(parts, axis):
    n = parts.shape[0] // 4
    return [parts[:n]] + [shift(parts[s * n : (s + 1) * n], axis, 4 - s) for s in range(1, 4)]


def back_two_steps(parts):
    n = parts.shape[0] // 4
    got = swap(parts[2 * n :], "co", 1, 2)
    pair = (parts[: 2 * n].astype(f32) + got.astype(f32)).astype(bf16)
    return [pair[:n], swap(pair[n:], "zl", 1, 2)]


def add_up(terms):
    a = [t.astype(f32) for t in terms]
    while len(a) > 1:
        a = [a[n] + a[n + 1] for n in range(0, len(a), 2)]
    return a[0]


def to_all(rows, axis):
    return lax.all_to_all(rows, axis, split_axis=0, concat_axis=0, tiled=True)


def reduce_cores(keep, give):
    return (keep.astype(f32) + swap(give, "co", 1, 2).astype(f32)).astype(bf16)


def gather_wide(wide):
    mine = to_all(wide, ("zl", "x", "y"))
    return mine.reshape((8, 4) + wide.shape[1:])


def norm_parts(values):
    center = values - jnp.mean(values, -1, keepdims=True)
    scale = lax.rsqrt(jnp.mean(center * center, -1, keepdims=True) + 1e-05)
    return center * scale, scale


def norm_back(grad, gain, xhat, scale):
    gx = grad * gain
    mean_gx = jnp.mean(gx, -1, keepdims=True)
    mean_gxx = jnp.mean(gx * xhat, -1, keepdims=True)
    return scale * (gx - mean_gx - xhat * mean_gxx)


def gelu_parts(u):
    c = 0.7978845608028654
    t = jnp.tanh(c * (u + 0.044715 * u * u * u))
    value = 0.5 * u * (1.0 + t)
    slope = 0.5 * (1.0 + t) + 0.5 * u * (1.0 - t * t) * c * (1.0 + 3.0 * 0.044715 * u * u)
    return value, slope


def columns_of(weight, start, size):
    return lax.dynamic_slice_in_dim(weight, start, size, 1)


def per_device(
    tokens, attn_gain, attn_shift, input_weight, query_bias, value_bias, output_weight,
    output_bias, mlp_gain, mlp_shift, hidden_weight, hidden_bias, return_weight, return_bias,
    block_order, cotangent,
):
    fi = lax.axis_index("fsdp")
    zi = lax.axis_index("zl")
    xi = lax.axis_index("x")
    yi = lax.axis_index("y")
    ci = lax.axis_index("co")
    rows, width = tokens.shape[1], tokens.shape[2]
    half = width // 2
    group = 4 * rows
    order = block_order.reshape(2, 4, 4, 2, 2)
    back = (4 - jnp.arange(4)) % 4
    ys = (yi + back) % 4
    xs = (xi + back) % 4
    low_shard = fi == 0

    def both_shards(own, peer):
        return jnp.concatenate(
            [jnp.where(low_shard, own, peer), jnp.where(low_shard, peer, own)], axis=0
        )

    def from_peer(rows_own):
        return swap(rows_own, ("fsdp", "zl"), 3, 4)

    tokens_own = tokens[0]
    tokens_all = gather_shifts(tokens_own, "y")
    in_own = jnp.concatenate(
        [columns_of(input_weight, t * width + yi * WIDTH, WIDTH) for t in range(3)], axis=1)
    in_own, small = lax.optimization_barrier((in_own, (
        attn_gain, attn_shift, query_bias, value_bias, output_bias, mlp_gain, mlp_shift,
        return_bias, lax.dynamic_slice_in_dim(hidden_bias, yi * half, half, 0),
    )))
    in_peer = from_peer(in_own)
    vectors = jnp.stack(small)
    vec_peer = from_peer(vectors)
    slices = jnp.concatenate([
        lax.dynamic_slice_in_dim(output_weight, (yi % 2) * WIDTH, WIDTH, 0),
        jnp.concatenate(
            [columns_of(hidden_weight, f * 4 * half + yi * half, half) for f in range(2)], axis=1),
        lax.dynamic_slice_in_dim(return_weight, yi * half, half, 0),
    ], axis=0)
    cot_own = cotangent[0]
    slices, cot_own, in_peer, tokens_all = lax.optimization_barrier(
        (slices, cot_own, in_peer, tokens_all)
    )
    peer = from_peer(slices)
    cot_all = gather_shifts(cot_own, "y")

    order = block_order.reshape(2, 4, 4, 2, 2)
    q_blocks = order[zi, :, :, ci][xs][:, ys].reshape(-1)
    k_blocks = jnp.stack(
        [order[zi ^ (s % 2), xi, :, ci ^ (s // 2)] for s in range(4)]
    )[:, ys].reshape(-1)
    plan = attention_plan(q_blocks, k_blocks)

    weight_in = both_shards(in_own, in_peer)
    vec = jnp.concatenate(
        [jnp.where(low_shard, vectors, vec_peer), jnp.where(low_shard, vec_peer, vectors)],
        axis=1).astype(f32)
    gain_one, shift_one, bias_q, bias_v, bias_out, gain_two, shift_two, bias_ret, bias_hid = [
        vec[i] for i in range(9)
    ]
    bias_q = lax.dynamic_slice_in_dim(bias_q, yi * WIDTH, WIDTH, 0)
    bias_v = lax.dynamic_slice_in_dim(bias_v, yi * WIDTH, WIDTH, 0)

    xhat_one, scale_one = norm_parts(tokens_all.astype(f32))
    norm_one = (xhat_one * gain_one + shift_one).astype(bf16)
    projected = nn(norm_one, weight_in) + jnp.concatenate(
        [bias_q, jnp.zeros((WIDTH,), f32), bias_v]
    )
    projected = projected.astype(bf16)
    kv_all = gather_swaps(projected[:, WIDTH:])
    q_all = gather_shifts(projected[:, :WIDTH], "x")

    partial = attention_forward(plan, q_all, kv_all)
    parts = back_shifts(partial, "x")
    cuts = (WIDTH, WIDTH + half)
    weight_out = jnp.where(fi == yi // 2, slices[: cuts[0]], peer[: cuts[0]])
    weight_hid = both_shards(slices[cuts[0] : cuts[1]], peer[cuts[0] : cuts[1]])
    weight_ret = both_shards(slices[cuts[1] :], peer[cuts[1] :])

    attended, attended_low, stats, branch = merge(parts, weight_out)

    middle = tokens_own.astype(f32) + add_up(back_shifts(branch, "y")) + bias_out
    xhat_two, scale_two = norm_parts(middle)
    norm_two = (xhat_two * gain_two + shift_two).astype(bf16)
    norm_two_all = gather_shifts(norm_two, "y")
    pre_act = nn(norm_two_all, weight_hid) + bias_hid
    acted, slope = gelu_parts(pre_act)
    acted = acted.astype(bf16)

    grad_pre = (nt(cot_all, weight_ret) * slope).astype(bf16)
    grad_norm_two = add_up(back_shifts(nt(grad_pre, weight_hid).astype(bf16), "y"))
    cot = cot_own.astype(f32)
    grad_middle = cot + norm_back(grad_norm_two, gain_two, xhat_two, scale_two)
    grad_branch = grad_middle.astype(bf16)
    core = ci.astype(jnp.int32)[None]
    early = reduce_cores(*mlp_grads(core, acted, cot_all, norm_two_all, grad_pre))
    branch_terms = [grad_branch] + [shift(grad_branch, "y", s) for s in range(1, 4)]
    wide = sum_wide(to_all(early, ("fsdp", "zl", "x")))
    wide, branch_terms[3] = lax.optimization_barrier((wide, branch_terms[3]))
    grad_branch_all = jnp.concatenate(branch_terms, axis=0)
    do_pack = grad_attended_packed(grad_branch_all, weight_out, attended, stats)

    rank = yi.astype(jnp.int32)[None]
    mid = mid_chunks(rank, attended_low, grad_branch_all, cot_own, grad_norm_two, xhat_two, grad_pre)
    early_mine = gather_wide(wide)
    do_all = gather_shifts(do_pack, "x")
    out_part = nn(acted, weight_ret).astype(bf16)
    out_part, mid, do_all = lax.optimization_barrier((out_part, mid, do_all))

    dq_part, dkv_part = attention_backward(plan, q_all, kv_all, do_all)
    early_mine, out_part, dq_part = lax.optimization_barrier((early_mine, out_part, dq_part))
    dkv_terms = back_two_steps(dkv_part)
    dq_terms = back_shifts(dq_part, "x")
    out_terms = back_shifts(out_part, "y")
    dq_terms, out_terms = lax.optimization_barrier((dq_terms, out_terms))
    keep, give, grad_norm_part = late_chunks(
        jnp.concatenate([rank, core]), dq_terms, dkv_terms, norm_one, xhat_one, weight_in, mid
    )
    late = to_all(reduce_cores(keep, give), ("fsdp", "zl", "x"))
    norm_terms = back_shifts(grad_norm_part, "y")

    where = jnp.stack([ci, fi]).astype(jnp.int32)
    early_other = swap(early_mine, "co", 1, 2)
    g_hid, g_ret = place_early(where, early_mine, early_other)
    late, norm_terms = lax.optimization_barrier((late, norm_terms))
    late_mine = gather_wide(sum_wide(late))

    layer_out = (middle + add_up(out_terms) + bias_ret).astype(bf16)[None]
    tokens_grad = grad_middle + norm_back(
        add_up(norm_terms), gain_one, xhat_one[:rows], scale_one[:rows]
    )
    tokens_grad = tokens_grad.astype(bf16)[None]
    late_mine, g_hid, g_ret, layer_out, tokens_grad = lax.optimization_barrier(
        (late_mine, g_hid, g_ret, layer_out, tokens_grad)
    )
    late_other = swap(late_mine, "co", 1, 2)
    flip = jnp.stack([1 - ci, fi]).astype(jnp.int32)
    g_in, g_out, g_vec = place_late(flip, late_other, place_late(where, late_mine))
    g_in = g_in.reshape(half, 12 * WIDTH)
    g_out = g_out.reshape(half, width)

    return (
        layer_out, tokens_grad, g_vec[0, 0, 0], g_vec[0, 1, 0], g_in, g_vec[1, 0, 0],
        g_vec[1, 1, 0], g_out, g_vec[1, 1, 1], g_vec[0, 1, 1], g_vec[1, 0, 1], g_hid,
        g_vec[2, 0, 4:].reshape(-1), g_ret, g_vec[0, 0, 1],
    )


def solution(mesh):
    fine = Mesh(mesh.devices.reshape(2, 2, 4, 4, 2), ("fsdp", "zl", "x", "y", "co"))
    seq = P("fsdp", CTX, None)
    vec = P("fsdp")
    mat = P("fsdp", None)
    return jax.shard_map(
        per_device,
        mesh=fine,
        in_specs=(seq, vec, vec, mat, vec, vec, mat, vec, vec, vec, mat, vec, mat, vec, P(), seq),
        out_specs=(seq, seq, vec, vec, mat, vec, vec, mat, vec, vec, vec, mat, vec, mat, vec),
        check_vma=False,
    )
```
